32 devices in a mesh: lat: 8 (over z, x), lon: 4 (over y, core).
Axes of the slice: x: 2, y: 2, z: 4, core: 2. Of those that a mesh axis runs over, the one named last changes fastest.
Arguments:
- grid_input: bfloat16 [8, 4, 720, 227], P('lat', 'lon'), may hold values from -6 to 6
- w_grid: bfloat16 [227, 512], replicated, may hold values from -0.375 to 0.375
- w_send: bfloat16 [512, 512], replicated, may hold values from -0.25 to 0.25
- to_sector: int32 [8, 4, 720, 1], P('lat', 'lon'), may hold values from 0 to 3; in each aligned block of 720 rows (0 to 719, 720 to 1439, ..., all dimensions but the last counted through in order) at most 360 rows name the same one
- to_node: int32 [8, 4, 720], P('lat', 'lon'), may hold values from 0 to 39
- w_node: bfloat16 [512, 512], replicated, may hold values from -0.25 to 0.25
- mesh_links: int32 [8, 4, 40, 6], P('lat', 'lon'), may hold values from 0 to 359
- w_source: bfloat16 [2, 512, 512], replicated, may hold values from -0.25 to 0.25
- w_target: bfloat16 [2, 512, 512], replicated, may hold values from -0.25 to 0.25
- w_update: bfloat16 [2, 512, 512], replicated, may hold values from -0.25 to 0.25
- w_decode: bfloat16 [512, 512], replicated, may hold values from -0.25 to 0.25
- w_output: bfloat16 [512, 227], replicated, may hold values from -0.25 to 0.25
Outputs:
- grid_output: bfloat16 [8, 4, 720, 227], P('lat', 'lon')
- mesh_state: bfloat16 [8, 4, 40, 512], P('lat', 'lon')
The draws below stay inside these ranges and needn't reach their ends.
Inputs may be any that keep to these rules, and one draw needn't show every extreme that they name: `to_sector`: among the 720 grid points of one device, at most 360 name one sector, a bound that some block reaches.
All inputs are finite; a program needn't handle non-finite values.
Results may differ from the reference program's by a relative error of at most 0.015.
Values may be sent and summed in bfloat16 or wider, within the bound.
A program may use at most 64 MiB of HBM per device.

```python
import math
import jax
import jax.numpy as jnp
import numpy as np
from jax import lax

L = 512
V = 227
GRID_DEV = 720
MESH_DEV = 40
KNBR = 6
PROC = 2
CAP = 360
N_LAT = 8
N_LON = 4


def set_ends(values, stream_key, low, high):
    longest = values.shape.index(max(values.shape))
    spots = []
    for shift in (0, 1):
        where = [jax.random.randint(jax.random.fold_in(stream_key, axis), (), 0, length) for axis, length in enumerate(values.shape)]
        where[longest] = (where[longest] + shift) % values.shape[longest]
        spots.append(tuple(where))
    return values.at[spots[0]].set(low).at[spots[1]].set(high)


def levels(key, dims, cuts, smallest, largest):
    loudness, own = 1.0, jax.random.fold_in(key, 6)
    for axis_at, blocks in cuts:
        heights = jnp.exp(jax.random.uniform(jax.random.fold_in(own, axis_at), (blocks,), jnp.float32, smallest / len(cuts), largest / len(cuts)))
        loudness = loudness * jnp.repeat(heights, dims[axis_at] // blocks).reshape([-1 if axis == axis_at else 1 for axis in range(len(dims))])
    return loudness


def assign_block(own_key, own, number, rows, count, top, reach, skew):
    ranking = jax.random.permutation(own_key, count)
    heavy_load, ordinary = load_shares(count, rows * top, reach, skew, True), load_shares(count, rows * top, reach, skew, False)
    places = jnp.arange(count)

    def named(lengths, turn):
        used = int((lengths > 0).sum())
        fixed = max(1, used // 4)
        passed = fixed + (places - fixed + turn * (used - fixed)) % max(1, count - fixed)
        return jnp.zeros((count,), jnp.int32).at[ranking[jnp.where(places < fixed, places, passed)]].set(jnp.asarray(lengths, jnp.int32))

    lengths = jnp.where(number % 4 == 0, named(heavy_load, number // 4), named(ordinary, number - number // 4 - 1))
    mixed = jax.random.permutation(jax.random.fold_in(own, 3), count)
    source_of, sink = mixed[0:count // 2 * 2:2], mixed[1:count // 2 * 2:2]
    margin = jnp.minimum(lengths[source_of] - 1, reach - lengths[sink]) // 2
    margin = jnp.where((source_of == ranking[0]) | (sink == ranking[0]) | (lengths[sink] == 0), 0, jnp.maximum(margin, 0))
    passed = jax.random.randint(jax.random.fold_in(own, 4), (count // 2,), 0, 1 << 20) % (margin + 1)
    lengths = lengths.at[source_of].add(-passed).at[sink].add(passed)
    items = jnp.searchsorted(jnp.cumsum(lengths), jnp.arange(rows * top), side="right").astype(jnp.int32)
    table = items.reshape(top, rows).T
    table = table[jax.random.permutation(jax.random.fold_in(own, 1), rows)]
    turn = jax.random.randint(jax.random.fold_in(own, 2), (rows, 1), 0, top)
    return jnp.take_along_axis(table, (jnp.arange(top)[None, :] + turn) % top, axis=1)


def load_shares(number_of, total, most, slope, full):
    portions = [(1 << 20) // math.isqrt(rank ** slope) + 1 for rank in range(1, number_of + 1)]
    largest = most if full else min(most, max(-(-total // number_of), total * portions[0] // sum(portions)))
    least = 1 if total - largest >= number_of - 1 else 0
    counts, surplus = [largest] + [least] * (number_of - 1), total - largest - least * (number_of - 1)
    while surplus > 0:
        movable = [i for i in range(1, number_of) if counts[i] < largest] or [i for i in range(1, number_of) if counts[i] < most]
        mass, remaining = sum([portions[i] for i in movable]), surplus
        for i in movable:
            more = min(most - counts[i], max(1, remaining * portions[i] // mass), surplus)
            counts[i] = counts[i] + more
            surplus = surplus - more
    return np.array(counts)


def normal_values(own_key, extent, scale, limit, pieces=(), held_as=jnp.bfloat16):
    gain = levels(own_key, extent, pieces, -0.22, 0.18) if pieces else 1.0
    values = jax.random.normal(own_key, extent, jnp.float32) * scale * gain
    return jnp.minimum(jnp.maximum(values, -limit), limit).astype(held_as)


def setup_inputs(seed: int = 0) -> dict:
    seeds = jax.random.split(jax.random.key(seed), 13)
    grid_input = normal_values(seeds[0], (N_LAT, N_LON, GRID_DEV, V), 1.0, 6.0, ((0, 8), (1, 4)))
    w_grid = normal_values(seeds[1], (V, L), V ** -0.5, 0.375)
    w_send = normal_values(seeds[2], (L, L), L ** -0.5, 0.25)
    to_sector_keys = jax.random.split(jax.random.fold_in(seeds[3], 1), N_LAT * N_LON * GRID_DEV // GRID_DEV)
    to_sector_turns = jax.random.permutation(jax.random.fold_in(seeds[3], 3), N_LAT * N_LON * GRID_DEV // GRID_DEV)
    to_sector = jax.vmap(lambda own, number: assign_block(jax.random.fold_in(seeds[3], 2), own, number, GRID_DEV, N_LON, 1, CAP, 2))(to_sector_keys, to_sector_turns).reshape((N_LAT, N_LON, GRID_DEV, 1))
    to_node = set_ends(jax.random.randint(seeds[4], (N_LAT, N_LON, GRID_DEV), 0, MESH_DEV), jax.random.fold_in(seeds[4], 1), 0, MESH_DEV - 1).astype(jnp.int32)
    w_node = normal_values(seeds[5], (L, L), L ** -0.5, 0.25)
    mesh_links = set_ends(jax.random.randint(seeds[6], (N_LAT, N_LON, MESH_DEV, KNBR), 0, 9 * MESH_DEV), jax.random.fold_in(seeds[6], 1), 0, (9 * MESH_DEV) - 1).astype(jnp.int32)
    w_source = normal_values(seeds[7], (PROC, L, L), L ** -0.5, 0.25)
    w_target = normal_values(seeds[8], (PROC, L, L), L ** -0.5, 0.25)
    w_update = normal_values(seeds[9], (PROC, L, L), L ** -0.5, 0.25)
    w_decode = normal_values(seeds[10], (L, L), L ** -0.5, 0.25)
    w_output = normal_values(seeds[11], (L, V), L ** -0.5, 0.25)
    return dict(grid_input=grid_input, w_grid=w_grid, w_send=w_send, to_sector=to_sector, to_node=to_node, w_node=w_node, mesh_links=mesh_links, w_source=w_source, w_target=w_target, w_update=w_update, w_decode=w_decode, w_output=w_output)


def layer_norm(values):
    center = values - lax.optimization_barrier(jnp.mean(values, -1, keepdims=True))
    spread = lax.optimization_barrier(jnp.mean(center * center, -1, keepdims=True))
    return center * lax.rsqrt(spread + 1e-05)

def reference(grid_input, w_grid, w_send, to_sector, to_node, w_node, mesh_links, w_source, w_target, w_update, w_decode, w_output):

    def embed(band_input):
        flat = band_input.reshape(-1, V)
        return jax.nn.silu(jnp.dot(flat, w_grid, preferred_element_type=jnp.float32)).astype(jnp.bfloat16)

    def encode_band(items):
        band_input, band_sector, band_node = items
        hidden = embed(band_input)
        message = jax.nn.silu(jnp.dot(hidden, w_send, preferred_element_type=jnp.float32)).astype(jnp.bfloat16)
        target = (band_sector[..., 0] * MESH_DEV + band_node).astype(jnp.int32)
        per_source = message.astype(jnp.float32).reshape(N_LON, GRID_DEV, L)

        def source_sums(rows, index):
            return jax.ops.segment_sum(rows, index, num_segments=N_LON * MESH_DEV)
        partial_value = jax.vmap(source_sums)(per_source, target).astype(jnp.bfloat16)
        gathered = lax.optimization_barrier(jnp.sum(partial_value.astype(jnp.float32), axis=0))
        normed = layer_norm(gathered).astype(jnp.bfloat16)
        state = jax.nn.silu(jnp.dot(normed, w_node, preferred_element_type=jnp.float32)).astype(jnp.bfloat16)
        return state.reshape(N_LON, MESH_DEV, L)
    state = lax.map(encode_band, (grid_input, to_sector, to_node))
    bands = jnp.arange(N_LAT, dtype=jnp.int32)
    for layer_index in range(PROC):
        sender = jnp.dot(state.reshape(-1, L), w_source[layer_index], preferred_element_type=jnp.float32).astype(jnp.bfloat16)
        padded = jnp.pad(sender.reshape(N_LAT, N_LON, MESH_DEV, L), ((1, 1), (0, 0), (0, 0), (0, 0)))

        def layer_band(band, padded=padded, layer_index=layer_index):
            block = lax.dynamic_slice_in_dim(padded, band, 3, 0)
            beside_all = jnp.stack([jnp.roll(block, 1, 1), block, jnp.roll(block, -1, 1)], axis=2)
            table = jnp.transpose(beside_all, (1, 0, 2, 3, 4)).reshape(N_LON, 9 * MESH_DEV, L)
            links = mesh_links[band]
            picked = jax.vmap(lambda rows, index: rows[index])(table, links)
            own = state[band]
            toward = jnp.dot(own.reshape(-1, L), w_target[layer_index], preferred_element_type=jnp.float32).reshape(N_LON, MESH_DEV, 1, L)
            summed = lax.optimization_barrier(jnp.sum(jax.nn.silu(picked.astype(jnp.float32) + toward), axis=2))
            lifted = layer_norm(summed).astype(jnp.bfloat16)
            change = jnp.dot(lifted.reshape(-1, L), w_update[layer_index], preferred_element_type=jnp.float32)
            return (own.astype(jnp.float32) + change.reshape(N_LON, MESH_DEV, L)).astype(jnp.bfloat16)
        state = lax.map(layer_band, bands)

    def decode_band(items):
        band_input, band_sector, band_node, band_state = items
        hidden = embed(band_input)
        reply = jax.nn.silu(jnp.dot(band_state.reshape(-1, L), w_decode, preferred_element_type=jnp.float32)).astype(jnp.bfloat16)
        target = (band_sector[..., 0] * MESH_DEV + band_node).reshape(-1)
        joined = (hidden.astype(jnp.float32) + reply[target].astype(jnp.float32)).astype(jnp.bfloat16)
        result = jnp.dot(joined, w_output, preferred_element_type=jnp.float32).astype(jnp.bfloat16)
        return result.reshape(N_LON, GRID_DEV, V)
    grid_output = lax.map(decode_band, (grid_input, to_sector, to_node, state))
    return (grid_output, state)
```

```python
import functools

import jax
import jax.numpy as jnp
from jax import lax
from jax.experimental import pallas as pl
from jax.experimental.pallas import tpu as pltpu
from jax.sharding import PartitionSpec as P

MESH = pl.DeviceIdType.MESH
BF16 = jnp.bfloat16


def silu(values):
    half = 0.5 * values
    return half + half * jnp.tanh(half)


def layer_norm(values):
    center = values - jnp.mean(values, -1, keepdims=True)
    spread = jnp.mean(center * center, -1, keepdims=True)
    return center * lax.rsqrt(spread + 1e-05)


def matmul(left, right, left_dim=1, right_dim=0):
    return lax.dot_general(
        left, right, (((left_dim,), (right_dim,)), ((), ())), preferred_element_type=jnp.float32
    )


def kernel(
    n_lat,
    n_lon,
    nodes,
    rows,
    chunk,
    x_hbm,
    wg_hbm,
    ws_hbm,
    sector_ref,
    node_ref,
    wn_hbm,
    links_ref,
    wsrc_hbm,
    wtgt_hbm,
    wupd_hbm,
    wdec_hbm,
    wout_hbm,
    out_ref,
    state_ref,
    x,
    wg,
    ws,
    wn,
    wsrc,
    wtgt,
    wupd,
    wdec,
    wout,
    hidden,
    message,
    part,
    part_in,
    table,
    reply_all,
    base,
    load_sem,
    part_send,
    part_recv,
    halo_send,
    halo_recv,
    reply_send,
    reply_recv,
):
    band = lax.axis_index("lat")
    sector = lax.axis_index("lon")
    points = x.shape[1]
    latent = ws.shape[0]
    layers = wsrc.shape[0]
    has_low = band > 0
    has_high = band < n_lat - 1

    loads = [
        pltpu.make_async_copy(source, target, load_sem.at[i])
        for i, (source, target) in enumerate(
            (
                (x_hbm, x),
                (wg_hbm, wg),
                (ws_hbm, ws),
                (wn_hbm, wn),
                (wsrc_hbm, wsrc),
                (wout_hbm, wout),
                (wtgt_hbm, wtgt),
                (wupd_hbm, wupd),
                (wdec_hbm, wdec),
            )
        )
    ]
    for load in loads:
        load.start()

    def beside(lat_step, lon_step):
        return (band + lat_step, lax.rem(sector + lon_step + n_lon, n_lon))

    barrier = pltpu.get_barrier_semaphore()
    for step in range(1, n_lon):
        pl.semaphore_signal(barrier, inc=1, device_id=beside(0, step), device_id_type=MESH)

    @pl.when(has_low)
    def _():
        for step in (-1, 0, 1):
            pl.semaphore_signal(barrier, inc=1, device_id=beside(-1, step), device_id_type=MESH)

    @pl.when(has_high)
    def _():
        for step in (-1, 0, 1):
            pl.semaphore_signal(barrier, inc=1, device_id=beside(1, step), device_id_type=MESH)

    zeros = jnp.zeros((3, rows, latent), BF16)

    @pl.when(band == 0)
    def _():
        for layer in range(layers):
            table[layer, 0:3] = zeros

    @pl.when(band == n_lat - 1)
    def _():
        for layer in range(layers):
            table[layer, 6:9] = zeros

    target = sector_ref[...] * rows + node_ref[...]
    total = n_lon * rows
    chosen = jnp.where(
        lax.broadcasted_iota(jnp.int32, (total, points), 0) == target, 1.0, 0.0
    ).astype(BF16)

    loads[0].wait()
    loads[1].wait()
    hidden[...] = silu(matmul(x[...], wg[...], 0, 0)).astype(BF16)
    loads[2].wait()
    for start in range(0, points, chunk):
        span = pl.ds(start, chunk)
        message[span, :] = silu(matmul(hidden[span, :], ws[...])).astype(BF16)
    part[...] = matmul(chosen, message[...]).astype(BF16).reshape(n_lon, rows, latent)

    inner = jnp.logical_and(has_low, has_high)

    @pl.when(inner)
    def _():
        pl.semaphore_wait(barrier, n_lon - 1 + 6)

    @pl.when(jnp.logical_not(inner))
    def _():
        pl.semaphore_wait(barrier, n_lon - 1 + 3)

    sends = []
    for step in range(1, n_lon):
        copy = pltpu.make_async_remote_copy(
            src_ref=part.at[lax.rem(sector + step, n_lon)],
            dst_ref=part_in.at[step - 1],
            send_sem=part_send.at[step - 1],
            recv_sem=part_recv.at[step - 1],
            device_id=beside(0, step),
            device_id_type=MESH,
        )
        copy.start()
        sends.append(copy)

    loads[5].wait()
    base[...] = matmul(wout[...], hidden[...], 1, 1)
    links = links_ref[...]
    links = links + (rows - nodes) * (links // nodes)
    degree = links.shape[0]
    links = jnp.swapaxes(links, 0, 1)
    filler = jnp.zeros((rows - nodes, 1), jnp.int32)
    pieces = []
    for k in range(degree):
        pieces += [links[:, k : k + 1], filler]
    links = jnp.concatenate(pieces, axis=0)
    wanted = jnp.where(
        lax.broadcasted_iota(jnp.int32, (degree * rows, 9 * rows), 1) == links, 1.0, 0.0
    ).astype(BF16)

    gathered = part[sector].astype(jnp.float32)
    loads[3].wait()
    for step in range(1, n_lon):
        sends[step - 1].wait_recv()
        gathered = gathered + part_in[step - 1].astype(jnp.float32)
    state = silu(matmul(layer_norm(gathered).astype(BF16), wn[...])).astype(BF16)

    def halo(layer, lat_step, lon_step):
        slot = (1 - lat_step) * 3 + (1 - lon_step)
        return pltpu.make_async_remote_copy(
            src_ref=table.at[layer, 4],
            dst_ref=table.at[layer, slot],
            send_sem=halo_send.at[layer, slot],
            recv_sem=halo_recv.at[layer, slot],
            device_id=beside(lat_step, lon_step),
            device_id_type=MESH,
        )

    loads[4].wait()
    for layer in range(layers):
        table[layer, 4] = matmul(state, wsrc[layer]).astype(BF16)

        @pl.when(has_low)
        def _():
            for lon_step in (-1, 0, 1):
                halo(layer, -1, lon_step).start()

        @pl.when(has_high)
        def _():
            for lon_step in (-1, 0, 1):
                halo(layer, 1, lon_step).start()

        for lon_step in (-1, 1):
            halo(layer, 0, lon_step).start()
        if layer == 0:
            loads[6].wait()
            loads[7].wait()
        toward = matmul(state, wtgt[layer])
        for lon_step in (-1, 1):
            halo(layer, 0, lon_step).wait_recv()

        @pl.when(has_low)
        def _():
            for lon_step in (-1, 0, 1):
                halo(layer, 1, lon_step).wait_recv()

        @pl.when(has_high)
        def _():
            for lon_step in (-1, 0, 1):
                halo(layer, -1, lon_step).wait_recv()

        picked = matmul(wanted, table[layer].reshape(9 * rows, latent))
        summed = silu(picked[0:rows] + toward)
        for k in range(1, degree):
            summed = summed + silu(picked[k * rows : (k + 1) * rows] + toward)
        lifted = layer_norm(summed).astype(BF16)
        state = (state.astype(jnp.float32) + matmul(lifted, wupd[layer])).astype(BF16)

    loads[8].wait()
    reply = silu(matmul(state, wdec[...])).astype(BF16)
    reply_all[sector] = matmul(reply, wout[...], 1, 1).astype(BF16)
    replies = []
    for step in range(1, n_lon):
        copy = pltpu.make_async_remote_copy(
            src_ref=reply_all.at[sector],
            dst_ref=reply_all.at[sector],
            send_sem=reply_send.at[step - 1],
            recv_sem=reply_recv.at[step - 1],
            device_id=beside(0, step),
            device_id_type=MESH,
        )
        copy.start()
        replies.append(copy)
    state_ref[...] = state[0:nodes]
    for copy in sends:
        copy.wait_send()
    for layer in range(layers):
        for lon_step in (-1, 1):
            halo(layer, 0, lon_step).wait_send()

        @pl.when(has_low)
        def _():
            for lon_step in (-1, 0, 1):
                halo(layer, -1, lon_step).wait_send()

        @pl.when(has_high)
        def _():
            for lon_step in (-1, 0, 1):
                halo(layer, 1, lon_step).wait_send()

    for step in range(1, n_lon):
        source = lax.rem(sector - step + n_lon, n_lon)
        pltpu.make_async_remote_copy(
            src_ref=reply_all.at[source],
            dst_ref=reply_all.at[source],
            send_sem=reply_send.at[step - 1],
            recv_sem=reply_recv.at[step - 1],
            device_id=beside(0, step),
            device_id_type=MESH,
        ).wait_recv()
    fetched = matmul(reply_all[...].reshape(total, -1), chosen, 0, 0)
    out_ref[...] = (base[...] + fetched).astype(BF16)
    for copy in replies:
        copy.wait_send()


def body(
    grid_input,
    w_grid,
    w_send,
    to_sector,
    to_node,
    w_node,
    mesh_links,
    w_source,
    w_target,
    w_update,
    w_decode,
    w_output,
):
    n_lat = lax.axis_size("lat")
    n_lon = lax.axis_size("lon")
    points, variables = grid_input.shape[2:]
    latent = w_send.shape[0]
    nodes = mesh_links.shape[2]
    layers = w_source.shape[0]
    rows = -(-nodes // 16) * 16
    chunk = points // 3 if points % 48 == 0 else points
    hbm = pl.BlockSpec(memory_space=pltpu.HBM)
    vmem = pl.BlockSpec(memory_space=pltpu.VMEM)
    square = pltpu.VMEM((latent, latent), BF16)
    cube = pltpu.VMEM((layers, latent, latent), BF16)
    result, state = pl.pallas_call(
        functools.partial(kernel, n_lat, n_lon, nodes, rows, chunk),
        out_shape=(
            jax.ShapeDtypeStruct((variables, points), BF16),
            jax.ShapeDtypeStruct((nodes, latent), BF16),
        ),
        in_specs=[hbm, hbm, hbm, vmem, vmem, hbm, vmem, hbm, hbm, hbm, hbm, hbm],
        out_specs=(vmem, vmem),
        scratch_shapes=[
            pltpu.VMEM((variables, points), BF16),
            pltpu.VMEM((variables, latent), BF16),
            square,
            square,
            cube,
            cube,
            cube,
            square,
            pltpu.VMEM((variables, latent), BF16),
            pltpu.VMEM((points, latent), BF16),
            pltpu.VMEM((points, latent), BF16),
            pltpu.VMEM((n_lon, rows, latent), BF16),
            pltpu.VMEM((n_lon - 1, rows, latent), BF16),
            pltpu.VMEM((layers, 9, rows, latent), BF16),
            pltpu.VMEM((n_lon, rows, variables), BF16),
            pltpu.VMEM((variables, points), jnp.float32),
            pltpu.SemaphoreType.DMA((9,)),
            pltpu.SemaphoreType.DMA((n_lon - 1,)),
            pltpu.SemaphoreType.DMA((n_lon - 1,)),
            pltpu.SemaphoreType.DMA((layers, 9)),
            pltpu.SemaphoreType.DMA((layers, 9)),
            pltpu.SemaphoreType.DMA((n_lon - 1,)),
            pltpu.SemaphoreType.DMA((n_lon - 1,)),
        ],
        compiler_params=pltpu.CompilerParams(
            collective_id=0, has_side_effects=True, vmem_limit_bytes=40 * 1024 * 1024
        ),
    )(
        jnp.swapaxes(grid_input.reshape(points, variables), 0, 1),
        w_grid,
        w_send,
        to_sector.reshape(1, points),
        to_node.reshape(1, points),
        w_node,
        jnp.swapaxes(mesh_links.reshape(nodes, -1), 0, 1),
        w_source,
        w_target,
        w_update,
        w_decode,
        jnp.swapaxes(w_output, 0, 1),
    )
    return (jnp.swapaxes(result, 0, 1).reshape(1, 1, points, variables), state.reshape(1, 1, nodes, latent))


def solution(mesh):
    placed = (
        P("lat", "lon", None, None),
        P(),
        P(),
        P("lat", "lon", None, None),
        P("lat", "lon", None),
        P(),
        P("lat", "lon", None, None),
        P(),
        P(),
        P(),
        P(),
        P(),
    )
    return jax.shard_map(
        body,
        mesh=mesh,
        in_specs=placed,
        out_specs=(P("lat", "lon", None, None), P("lat", "lon", None, None)),
        check_vma=False,
    )
```

```python
import functools

import jax
import jax.numpy as jnp
from jax import lax
from jax.experimental import pallas as pl
from jax.experimental.pallas import tpu as pltpu
from jax.sharding import PartitionSpec as P

MESH = pl.DeviceIdType.MESH
BF16 = jnp.bfloat16
RELAYED = ()
LIMIT = 56


def silu(values):
    half = 0.5 * values
    return half + half * jnp.tanh(half)


def layer_norm(values):
    center = values - jnp.mean(values, -1, keepdims=True)
    spread = jnp.mean(center * center, -1, keepdims=True)
    return center * lax.rsqrt(spread + 1e-05)


def matmul(left, right, left_dim=1, right_dim=0):
    return lax.dot_general(
        left, right, (((left_dim,), (right_dim,)), ((), ())), preferred_element_type=jnp.float32
    )


def kernel(
    n_lat,
    n_lon,
    relayed,
    chunk,
    x_hbm,
    wg_hbm,
    ws_hbm,
    sector_hbm,
    node_hbm,
    wn_hbm,
    links_hbm,
    wsrc_hbm,
    wtgt_hbm,
    wupd_hbm,
    wdec_hbm,
    wout_hbm,
    out_ref,
    state_ref,
    x,
    wg,
    ws,
    sector_of,
    node_of,
    wn,
    links_of,
    wsrc,
    wtgt,
    wupd,
    wdec,
    wout,
    hidden,
    message,
    part,
    part_in,
    table,
    reply_all,
    base,
    load_sem,
    part_send,
    part_recv,
    halo_send,
    halo_recv,
    reply_send,
    reply_recv,
):
    band = lax.axis_index("lat")
    sector = lax.axis_index("lon")
    points = x.shape[1]
    latent = ws.shape[0]
    half = latent // 2
    layers = wsrc.shape[0]
    nodes = state_ref.shape[0]
    rows = reply_all.shape[1]
    has_low = band > 0
    has_high = band < n_lat - 1
    side = 1 - 2 * lax.rem(sector, 2)
    columns = (0, side, -side)

    loads = [
        pltpu.make_async_copy(source, target, load_sem.at[i])
        for i, (source, target) in enumerate(
            (
                (x_hbm, x),
                (wg_hbm, wg),
                (ws_hbm, ws),
                (sector_hbm, sector_of),
                (node_hbm, node_of),
                (links_hbm, links_of),
                (wout_hbm, wout),
                (wn_hbm, wn),
                (wsrc_hbm, wsrc),
                (wtgt_hbm, wtgt),
                (wupd_hbm, wupd),
                (wdec_hbm, wdec),
            )
        )
    ]
    for load in loads:
        load.start()

    def beside(lat_step, lon_step):
        return (band + lat_step, lax.rem(sector + lon_step + n_lon, n_lon))

    direct = [column for column in (0, 2, 1) if column not in relayed]
    barrier = pltpu.get_barrier_semaphore()
    for step in range(1, n_lon):
        pl.semaphore_signal(barrier, inc=1, device_id=beside(0, step), device_id_type=MESH)

    @pl.when(has_low)
    def _():
        for column in direct:
            pl.semaphore_signal(
                barrier, inc=1, device_id=beside(-1, columns[column]), device_id_type=MESH
            )

    @pl.when(has_high)
    def _():
        for column in direct:
            pl.semaphore_signal(
                barrier, inc=1, device_id=beside(1, columns[column]), device_id_type=MESH
            )

    zeros = jnp.zeros((3, 2 * nodes, half), BF16)

    @pl.when(band == 0)
    def _():
        for layer in range(layers):
            table[layer, 0:3] = zeros

    @pl.when(band == n_lat - 1)
    def _():
        for layer in range(layers):
            table[layer, 6:9] = zeros

    loads[0].wait()
    loads[1].wait()
    hidden[...] = silu(matmul(x[...], wg[...], 0, 0)).astype(BF16)
    loads[2].wait()
    for start in range(0, points, chunk):
        span = pl.ds(start, chunk)
        message[span, :] = silu(matmul(hidden[span, :], ws[...])).astype(BF16)
    loads[3].wait()
    loads[4].wait()
    target = sector_of[...] * nodes + node_of[...]
    chosen = jnp.where(
        lax.broadcasted_iota(jnp.int32, (n_lon * nodes, points), 0) == target, 1.0, 0.0
    ).astype(BF16)
    partial = matmul(chosen, message[...])
    for other in range(n_lon):
        block = partial[other * nodes : (other + 1) * nodes]
        part[other] = jnp.concatenate([block[:, :half], block[:, half:]], axis=0).astype(BF16)

    inner = jnp.logical_and(has_low, has_high)

    @pl.when(inner)
    def _():
        pl.semaphore_wait(barrier, n_lon - 1 + 2 * len(direct))

    @pl.when(jnp.logical_not(inner))
    def _():
        pl.semaphore_wait(barrier, n_lon - 1 + len(direct))

    sends = []
    for step in range(1, n_lon):
        copy = pltpu.make_async_remote_copy(
            src_ref=part.at[lax.rem(sector + step, n_lon)],
            dst_ref=part_in.at[step - 1],
            send_sem=part_send.at[step - 1],
            recv_sem=part_recv.at[step - 1],
            device_id=beside(0, step),
            device_id_type=MESH,
        )
        copy.start()
        sends.append(copy)

    loads[5].wait()
    loads[6].wait()
    base[...] = matmul(wout[...], hidden[...], 1, 1)
    degree = links_of.shape[0]
    links = jnp.swapaxes(jnp.concatenate([links_of[k] for k in range(degree)], axis=0), 0, 1)
    links = jnp.concatenate([links[:, k : k + 1] for k in range(degree)], axis=0)
    cell = links // nodes
    lon_step = cell % 3 - 1
    column = jnp.where(lon_step == 0, 0, jnp.where(lon_step == side, 1, 2))
    links = links - cell * nodes + ((cell // 3) * 3 + column) * (2 * nodes)
    slots = lax.broadcasted_iota(jnp.int32, (degree * nodes, 18 * nodes), 1)
    wanted_low = jnp.where(slots == links, 1.0, 0.0).astype(BF16)
    wanted_high = jnp.where(slots == links + nodes, 1.0, 0.0).astype(BF16)
    answered = sector_of[...] * rows + node_of[...]
    fetching = jnp.where(
        lax.broadcasted_iota(jnp.int32, (n_lon * rows, points), 0) == answered, 1.0, 0.0
    ).astype(BF16)

    gathered = part[sector].astype(jnp.float32)
    for load in loads[7:]:
        load.wait()
    for step in range(1, n_lon):
        sends[step - 1].wait_recv()
        gathered = gathered + part_in[step - 1].astype(jnp.float32)
    gathered = jnp.concatenate([gathered[:nodes], gathered[nodes:]], axis=1)
    state = silu(matmul(layer_norm(gathered).astype(BF16), wn[...])).astype(BF16)

    def halo(layer, lat_step, column, source=3):
        slot = (1 - lat_step) * 3 + column
        return pltpu.make_async_remote_copy(
            src_ref=table.at[layer, source],
            dst_ref=table.at[layer, slot],
            send_sem=halo_send.at[layer, slot],
            recv_sem=halo_recv.at[layer, slot],
            device_id=beside(lat_step, columns[column]),
            device_id_type=MESH,
        )

    def forward(layer, row, column):
        slot = row * 3 + column
        return pltpu.make_async_remote_copy(
            src_ref=table.at[layer, row * 3],
            dst_ref=table.at[layer, slot],
            send_sem=halo_send.at[layer, slot],
            recv_sem=halo_recv.at[layer, slot],
            device_id=beside(0, columns[column]),
            device_id_type=MESH,
        )

    for layer in range(layers):
        own = matmul(state, wsrc[layer])
        table[layer, 3] = jnp.concatenate([own[:, :half], own[:, half:]], axis=0).astype(BF16)

        @pl.when(has_high)
        def _():
            for column in direct:
                halo(layer, 1, column).start()

        @pl.when(has_low)
        def _():
            for column in direct:
                halo(layer, -1, column).start()

        for column in (2, 1):
            halo(layer, 0, column).start()
        toward = matmul(state, wtgt[layer])

        @pl.when(has_low)
        def _():
            halo(layer, 1, 0).wait_recv()
            for column in relayed:
                forward(layer, 0, column).start()

        @pl.when(has_high)
        def _():
            halo(layer, -1, 0).wait_recv()
            for column in relayed:
                forward(layer, 2, column).start()

        for column in (1, 2):
            halo(layer, 0, column).wait_recv()

        @pl.when(has_low)
        def _():
            for column in (2, 1):
                halo(layer, 1, column).wait_recv()

        @pl.when(has_high)
        def _():
            for column in (2, 1):
                halo(layer, -1, column).wait_recv()

        senders = table[layer].reshape(18 * nodes, half)
        picked = jnp.concatenate(
            [matmul(wanted_low, senders), matmul(wanted_high, senders)], axis=1
        )
        summed = silu(picked[0:nodes] + toward)
        for k in range(1, degree):
            summed = summed + silu(picked[k * nodes : (k + 1) * nodes] + toward)
        lifted = layer_norm(summed).astype(BF16)
        state = (state.astype(jnp.float32) + matmul(lifted, wupd[layer])).astype(BF16)

    reply = silu(matmul(state, wdec[...])).astype(BF16)
    reply = matmul(reply, wout[...], 1, 1)
    if rows > nodes:
        filler = jnp.zeros((rows - nodes, reply.shape[1]), jnp.float32)
        reply = jnp.concatenate([reply, filler], axis=0)
    reply_all[sector] = reply.astype(BF16)
    replies = []
    for step in range(1, n_lon):
        copy = pltpu.make_async_remote_copy(
            src_ref=reply_all.at[sector],
            dst_ref=reply_all.at[sector],
            send_sem=reply_send.at[step - 1],
            recv_sem=reply_recv.at[step - 1],
            device_id=beside(0, step),
            device_id_type=MESH,
        )
        copy.start()
        replies.append(copy)
    state_ref[...] = state
    for copy in sends:
        copy.wait_send()
    for layer in range(layers):
        for column in (1, 2):
            halo(layer, 0, column).wait_send()

        @pl.when(has_low)
        def _():
            for column in direct:
                halo(layer, -1, column).wait_send()
            for column in relayed:
                forward(layer, 0, column).wait_send()

        @pl.when(has_high)
        def _():
            for column in direct:
                halo(layer, 1, column).wait_send()
            for column in relayed:
                forward(layer, 2, column).wait_send()

    for step in range(1, n_lon):
        source = lax.rem(sector - step + n_lon, n_lon)
        pltpu.make_async_remote_copy(
            src_ref=reply_all.at[source],
            dst_ref=reply_all.at[source],
            send_sem=reply_send.at[step - 1],
            recv_sem=reply_recv.at[step - 1],
            device_id=beside(0, step),
            device_id_type=MESH,
        ).wait_recv()
    fetched = matmul(reply_all[...].reshape(n_lon * rows, -1), fetching, 0, 0)
    out_ref[...] = (base[...] + fetched).astype(BF16)
    for copy in replies:
        copy.wait_send()


def body(
    grid_input,
    w_grid,
    w_send,
    to_sector,
    to_node,
    w_node,
    mesh_links,
    w_source,
    w_target,
    w_update,
    w_decode,
    w_output,
):
    n_lat = lax.axis_size("lat")
    n_lon = lax.axis_size("lon")
    points, variables = grid_input.shape[2:]
    latent = w_send.shape[0]
    nodes = mesh_links.shape[2]
    layers = w_source.shape[0]
    rows = -(-nodes // 16) * 16
    chunk = points // 3 if points % 48 == 0 else points
    hbm = pl.BlockSpec(memory_space=pltpu.HBM)
    vmem = pl.BlockSpec(memory_space=pltpu.VMEM)
    square = pltpu.VMEM((latent, latent), BF16)
    cube = pltpu.VMEM((layers, latent, latent), BF16)
    result, state = pl.pallas_call(
        functools.partial(kernel, n_lat, n_lon, RELAYED, chunk),
        out_shape=(
            jax.ShapeDtypeStruct((variables, points), BF16),
            jax.ShapeDtypeStruct((nodes, latent), BF16),
        ),
        in_specs=[hbm] * 12,
        out_specs=(vmem, vmem),
        scratch_shapes=[
            pltpu.VMEM((variables, points), BF16),
            pltpu.VMEM((variables, latent), BF16),
            square,
            pltpu.VMEM((1, points), jnp.int32),
            pltpu.VMEM((1, points), jnp.int32),
            square,
            pltpu.VMEM((mesh_links.shape[3], 1, nodes), jnp.int32),
            cube,
            cube,
            cube,
            square,
            pltpu.VMEM((variables, latent), BF16),
            pltpu.VMEM((points, latent), BF16),
            pltpu.VMEM((points, latent), BF16),
            pltpu.VMEM((n_lon, 2 * nodes, latent // 2), BF16),
            pltpu.VMEM((n_lon - 1, 2 * nodes, latent // 2), BF16),
            pltpu.VMEM((layers, 9, 2 * nodes, latent // 2), BF16),
            pltpu.VMEM((n_lon, rows, variables), BF16),
            pltpu.VMEM((variables, points), jnp.float32),
            pltpu.SemaphoreType.DMA((12,)),
            pltpu.SemaphoreType.DMA((n_lon - 1,)),
            pltpu.SemaphoreType.DMA((n_lon - 1,)),
            pltpu.SemaphoreType.DMA((layers, 9)),
            pltpu.SemaphoreType.DMA((layers, 9)),
            pltpu.SemaphoreType.DMA((n_lon - 1,)),
            pltpu.SemaphoreType.DMA((n_lon - 1,)),
        ],
        compiler_params=pltpu.CompilerParams(
            collective_id=0, has_side_effects=True, vmem_limit_bytes=LIMIT * 1024 * 1024
        ),
    )(
        jnp.swapaxes(grid_input.reshape(points, variables), 0, 1),
        w_grid,
        w_send,
        to_sector.reshape(1, points),
        to_node.reshape(1, points),
        w_node,
        jnp.transpose(mesh_links, (0, 3, 1, 2)).reshape(-1, 1, nodes),
        w_source,
        w_target,
        w_update,
        w_decode,
        jnp.swapaxes(w_output, 0, 1),
    )
    return (jnp.swapaxes(result, 0, 1).reshape(1, 1, points, variables), state.reshape(1, 1, nodes, latent))


def solution(mesh):
    placed = (
        P("lat", "lon", None, None),
        P(),
        P(),
        P("lat", "lon", None, None),
        P("lat", "lon", None),
        P(),
        P("lat", "lon", None, None),
        P(),
        P(),
        P(),
        P(),
        P(),
    )
    return jax.shard_map(
        body,
        mesh=mesh,
        in_specs=placed,
        out_specs=(P("lat", "lon", None, None), P("lat", "lon", None, None)),
        check_vma=False,
    )
```

```python
import functools

import jax
import jax.numpy as jnp
from jax import lax
from jax.experimental import pallas as pl
from jax.experimental.pallas import tpu as pltpu
from jax.sharding import PartitionSpec as P

MESH = pl.DeviceIdType.MESH
BF16 = jnp.bfloat16
RELAYED = (1,)
LIMIT = 56


def silu(values):
    half = 0.5 * values
    return half + half * jnp.tanh(half)


def layer_norm(values):
    center = values - jnp.mean(values, -1, keepdims=True)
    spread = jnp.mean(center * center, -1, keepdims=True)
    return center * lax.rsqrt(spread + 1e-05)


def matmul(left, right, left_dim=1, right_dim=0):
    return lax.dot_general(
        left, right, (((left_dim,), (right_dim,)), ((), ())), preferred_element_type=jnp.float32
    )


def kernel(
    n_lat,
    n_lon,
    relayed,
    chunk,
    x_hbm,
    wg_hbm,
    ws_hbm,
    sector_hbm,
    node_hbm,
    wn_hbm,
    links_hbm,
    wsrc_hbm,
    wtgt_hbm,
    wupd_hbm,
    wdec_hbm,
    wout_hbm,
    out_ref,
    state_ref,
    x,
    wg,
    ws,
    sector_of,
    node_of,
    wn,
    links_of,
    wsrc,
    wtgt,
    wupd,
    wdec,
    wout,
    hidden,
    message,
    part,
    part_in,
    table,
    reply_all,
    base,
    load_sem,
    part_send,
    part_recv,
    halo_send,
    halo_recv,
    reply_send,
    reply_recv,
):
    band = lax.axis_index("lat")
    sector = lax.axis_index("lon")
    points = x.shape[1]
    latent = ws.shape[0]
    half = latent // 2
    layers = wsrc.shape[0]
    nodes = state_ref.shape[0]
    rows = reply_all.shape[1]
    has_low = band > 0
    has_high = band < n_lat - 1
    side = 1 - 2 * lax.rem(sector, 2)
    columns = (0, side, -side)

    loads = [
        pltpu.make_async_copy(source, target, load_sem.at[i])
        for i, (source, target) in enumerate(
            (
                (x_hbm, x),
                (wg_hbm, wg),
                (ws_hbm, ws),
                (sector_hbm, sector_of),
                (node_hbm, node_of),
                (links_hbm, links_of),
                (wout_hbm, wout),
                (wn_hbm, wn),
                (wsrc_hbm, wsrc),
                (wtgt_hbm, wtgt),
                (wupd_hbm, wupd),
                (wdec_hbm, wdec),
            )
        )
    ]
    for load in loads:
        load.start()

    def beside(lat_step, lon_step):
        return (band + lat_step, lax.rem(sector + lon_step + n_lon, n_lon))

    direct = [column for column in (0, 2, 1) if column not in relayed]
    barrier = pltpu.get_barrier_semaphore()
    for step in range(1, n_lon):
        pl.semaphore_signal(barrier, inc=1, device_id=beside(0, step), device_id_type=MESH)

    @pl.when(has_low)
    def _():
        for column in direct:
            pl.semaphore_signal(
                barrier, inc=1, device_id=beside(-1, columns[column]), device_id_type=MESH
            )

    @pl.when(has_high)
    def _():
        for column in direct:
            pl.semaphore_signal(
                barrier, inc=1, device_id=beside(1, columns[column]), device_id_type=MESH
            )

    zeros = jnp.zeros((3, 2 * nodes, half), BF16)

    @pl.when(band == 0)
    def _():
        for layer in range(layers):
            table[layer, 0:3] = zeros

    @pl.when(band == n_lat - 1)
    def _():
        for layer in range(layers):
            table[layer, 6:9] = zeros

    loads[0].wait()
    loads[1].wait()
    hidden[...] = silu(matmul(x[...], wg[...], 0, 0)).astype(BF16)
    loads[2].wait()
    for start in range(0, points, chunk):
        span = pl.ds(start, chunk)
        message[span, :] = silu(matmul(hidden[span, :], ws[...])).astype(BF16)
    loads[3].wait()
    loads[4].wait()
    target = sector_of[...] * nodes + node_of[...]
    chosen = jnp.where(
        lax.broadcasted_iota(jnp.int32, (n_lon * nodes, points), 0) == target, 1.0, 0.0
    ).astype(BF16)
    partial = matmul(chosen, message[...])
    for other in range(n_lon):
        block = partial[other * nodes : (other + 1) * nodes]
        part[other] = jnp.concatenate([block[:, :half], block[:, half:]], axis=0).astype(BF16)

    inner = jnp.logical_and(has_low, has_high)

    @pl.when(inner)
    def _():
        pl.semaphore_wait(barrier, n_lon - 1 + 2 * len(direct))

    @pl.when(jnp.logical_not(inner))
    def _():
        pl.semaphore_wait(barrier, n_lon - 1 + len(direct))

    sends = []
    for step in range(1, n_lon):
        copy = pltpu.make_async_remote_copy(
            src_ref=part.at[lax.rem(sector + step, n_lon)],
            dst_ref=part_in.at[step - 1],
            send_sem=part_send.at[step - 1],
            recv_sem=part_recv.at[step - 1],
            device_id=beside(0, step),
            device_id_type=MESH,
        )
        copy.start()
        sends.append(copy)

    loads[5].wait()
    loads[6].wait()
    base[...] = matmul(wout[...], hidden[...], 1, 1)
    degree = links_of.shape[0]
    links = jnp.swapaxes(jnp.concatenate([links_of[k] for k in range(degree)], axis=0), 0, 1)
    links = jnp.concatenate([links[:, k : k + 1] for k in range(degree)], axis=0)
    cell = links // nodes
    lon_step = cell % 3 - 1
    column = jnp.where(lon_step == 0, 0, jnp.where(lon_step == side, 1, 2))
    links = links - cell * nodes + ((cell // 3) * 3 + column) * (2 * nodes)
    slots = lax.broadcasted_iota(jnp.int32, (degree * nodes, 18 * nodes), 1)
    wanted_low = jnp.where(slots == links, 1.0, 0.0).astype(BF16)
    wanted_high = jnp.where(slots == links + nodes, 1.0, 0.0).astype(BF16)
    answered = sector_of[...] * rows + node_of[...]
    fetching = jnp.where(
        lax.broadcasted_iota(jnp.int32, (n_lon * rows, points), 0) == answered, 1.0, 0.0
    ).astype(BF16)

    gathered = part[sector].astype(jnp.float32)
    for load in loads[7:]:
        load.wait()
    for step in range(1, n_lon):
        sends[step - 1].wait_recv()
        gathered = gathered + part_in[step - 1].astype(jnp.float32)
    gathered = jnp.concatenate([gathered[:nodes], gathered[nodes:]], axis=1)
    state = silu(matmul(layer_norm(gathered).astype(BF16), wn[...])).astype(BF16)

    def halo(layer, lat_step, column, source=3):
        slot = (1 - lat_step) * 3 + column
        return pltpu.make_async_remote_copy(
            src_ref=table.at[layer, source],
            dst_ref=table.at[layer, slot],
            send_sem=halo_send.at[layer, slot],
            recv_sem=halo_recv.at[layer, slot],
            device_id=beside(lat_step, columns[column]),
            device_id_type=MESH,
        )

    def forward(layer, row, column):
        slot = row * 3 + column
        return pltpu.make_async_remote_copy(
            src_ref=table.at[layer, row * 3],
            dst_ref=table.at[layer, slot],
            send_sem=halo_send.at[layer, slot],
            recv_sem=halo_recv.at[layer, slot],
            device_id=beside(0, columns[column]),
            device_id_type=MESH,
        )

    for layer in range(layers):
        own = matmul(state, wsrc[layer])
        table[layer, 3] = jnp.concatenate([own[:, :half], own[:, half:]], axis=0).astype(BF16)

        @pl.when(has_high)
        def _():
            for column in direct:
                halo(layer, 1, column).start()

        @pl.when(has_low)
        def _():
            for column in direct:
                halo(layer, -1, column).start()

        for column in (2, 1):
            halo(layer, 0, column).start()
        toward = matmul(state, wtgt[layer])

        @pl.when(has_low)
        def _():
            halo(layer, 1, 0).wait_recv()
            for column in relayed:
                forward(layer, 0, column).start()

        @pl.when(has_high)
        def _():
            halo(layer, -1, 0).wait_recv()
            for column in relayed:
                forward(layer, 2, column).start()

        for column in (1, 2):
            halo(layer, 0, column).wait_recv()

        @pl.when(has_low)
        def _():
            for column in (2, 1):
                halo(layer, 1, column).wait_recv()

        @pl.when(has_high)
        def _():
            for column in (2, 1):
                halo(layer, -1, column).wait_recv()

        senders = table[layer].reshape(18 * nodes, half)
        picked = jnp.concatenate(
            [matmul(wanted_low, senders), matmul(wanted_high, senders)], axis=1
        )
        summed = silu(picked[0:nodes] + toward)
        for k in range(1, degree):
            summed = summed + silu(picked[k * nodes : (k + 1) * nodes] + toward)
        lifted = layer_norm(summed).astype(BF16)
        state = (state.astype(jnp.float32) + matmul(lifted, wupd[layer])).astype(BF16)

    reply = silu(matmul(state, wdec[...])).astype(BF16)
    reply = matmul(reply, wout[...], 1, 1)
    if rows > nodes:
        filler = jnp.zeros((rows - nodes, reply.shape[1]), jnp.float32)
        reply = jnp.concatenate([reply, filler], axis=0)
    reply_all[sector] = reply.astype(BF16)
    replies = []
    for step in range(1, n_lon):
        copy = pltpu.make_async_remote_copy(
            src_ref=reply_all.at[sector],
            dst_ref=reply_all.at[sector],
            send_sem=reply_send.at[step - 1],
            recv_sem=reply_recv.at[step - 1],
            device_id=beside(0, step),
            device_id_type=MESH,
        )
        copy.start()
        replies.append(copy)
    state_ref[...] = state
    for copy in sends:
        copy.wait_send()
    for layer in range(layers):
        for column in (1, 2):
            halo(layer, 0, column).wait_send()

        @pl.when(has_low)
        def _():
            for column in direct:
                halo(layer, -1, column).wait_send()
            for column in relayed:
                forward(layer, 0, column).wait_send()

        @pl.when(has_high)
        def _():
            for column in direct:
                halo(layer, 1, column).wait_send()
            for column in relayed:
                forward(layer, 2, column).wait_send()

    for step in range(1, n_lon):
        source = lax.rem(sector - step + n_lon, n_lon)
        pltpu.make_async_remote_copy(
            src_ref=reply_all.at[source],
            dst_ref=reply_all.at[source],
            send_sem=reply_send.at[step - 1],
            recv_sem=reply_recv.at[step - 1],
            device_id=beside(0, step),
            device_id_type=MESH,
        ).wait_recv()
    fetched = matmul(reply_all[...].reshape(n_lon * rows, -1), fetching, 0, 0)
    out_ref[...] = (base[...] + fetched).astype(BF16)
    for copy in replies:
        copy.wait_send()


def body(
    grid_input,
    w_grid,
    w_send,
    to_sector,
    to_node,
    w_node,
    mesh_links,
    w_source,
    w_target,
    w_update,
    w_decode,
    w_output,
):
    n_lat = lax.axis_size("lat")
    n_lon = lax.axis_size("lon")
    points, variables = grid_input.shape[2:]
    latent = w_send.shape[0]
    nodes = mesh_links.shape[2]
    layers = w_source.shape[0]
    rows = -(-nodes // 16) * 16
    chunk = points // 3 if points % 48 == 0 else points
    hbm = pl.BlockSpec(memory_space=pltpu.HBM)
    vmem = pl.BlockSpec(memory_space=pltpu.VMEM)
    square = pltpu.VMEM((latent, latent), BF16)
    cube = pltpu.VMEM((layers, latent, latent), BF16)
    result, state = pl.pallas_call(
        functools.partial(kernel, n_lat, n_lon, RELAYED, chunk),
        out_shape=(
            pltpu.VMEM((variables, points), BF16),
            pltpu.VMEM((nodes, latent), BF16),
        ),
        in_specs=[hbm] * 12,
        out_specs=(vmem, vmem),
        scratch_shapes=[
            pltpu.VMEM((variables, points), BF16),
            pltpu.VMEM((variables, latent), BF16),
            square,
            pltpu.VMEM((1, points), jnp.int32),
            pltpu.VMEM((1, points), jnp.int32),
            square,
            pltpu.VMEM((mesh_links.shape[3], 1, nodes), jnp.int32),
            cube,
            cube,
            cube,
            square,
            pltpu.VMEM((variables, latent), BF16),
            pltpu.VMEM((points, latent), BF16),
            pltpu.VMEM((points, latent), BF16),
            pltpu.VMEM((n_lon, 2 * nodes, latent // 2), BF16),
            pltpu.VMEM((n_lon - 1, 2 * nodes, latent // 2), BF16),
            pltpu.VMEM((layers, 9, 2 * nodes, latent // 2), BF16),
            pltpu.VMEM((n_lon, rows, variables), BF16),
            pltpu.VMEM((variables, points), jnp.float32),
            pltpu.SemaphoreType.DMA((12,)),
            pltpu.SemaphoreType.DMA((n_lon - 1,)),
            pltpu.SemaphoreType.DMA((n_lon - 1,)),
            pltpu.SemaphoreType.DMA((layers, 9)),
            pltpu.SemaphoreType.DMA((layers, 9)),
            pltpu.SemaphoreType.DMA((n_lon - 1,)),
            pltpu.SemaphoreType.DMA((n_lon - 1,)),
        ],
        compiler_params=pltpu.CompilerParams(
            collective_id=0, has_side_effects=True, vmem_limit_bytes=LIMIT * 1024 * 1024
        ),
    )(
        jnp.swapaxes(grid_input.reshape(points, variables), 0, 1),
        w_grid,
        w_send,
        to_sector.reshape(1, points),
        to_node.reshape(1, points),
        w_node,
        jnp.transpose(mesh_links, (0, 3, 1, 2)).reshape(-1, 1, nodes),
        w_source,
        w_target,
        w_update,
        w_decode,
        jnp.swapaxes(w_output, 0, 1),
    )
    return (jnp.swapaxes(result, 0, 1).reshape(1, 1, points, variables), state.reshape(1, 1, nodes, latent))


def solution(mesh):
    placed = (
        P("lat", "lon", None, None),
        P(),
        P(),
        P("lat", "lon", None, None),
        P("lat", "lon", None),
        P(),
        P("lat", "lon", None, None),
        P(),
        P(),
        P(),
        P(),
        P(),
    )
    return jax.shard_map(
        body,
        mesh=mesh,
        in_specs=placed,
        out_specs=(P("lat", "lon", None, None), P("lat", "lon", None, None)),
        check_vma=False,
    )
```

```python
import functools

import jax
import jax.numpy as jnp
from jax import lax
from jax.experimental import pallas as pl
from jax.experimental.pallas import tpu as pltpu
from jax.sharding import PartitionSpec as P

MESH = pl.DeviceIdType.MESH
BF16 = jnp.bfloat16
RELAYED = (1,)
LIMIT = 56


def silu(values):
    half = 0.5 * values
    return half + half * jnp.tanh(half)


def layer_norm(values):
    center = values - jnp.mean(values, -1, keepdims=True)
    spread = jnp.mean(center * center, -1, keepdims=True)
    return center * lax.rsqrt(spread + 1e-05)


def matmul(left, right, left_dim=1, right_dim=0):
    return lax.dot_general(
        left, right, (((left_dim,), (right_dim,)), ((), ())), preferred_element_type=jnp.float32
    )


def kernel(
    n_lat,
    n_lon,
    relayed,
    chunk,
    x_hbm,
    wg_hbm,
    ws_hbm,
    sector_hbm,
    node_hbm,
    wn_hbm,
    links_hbm,
    wsrc_hbm,
    wtgt_hbm,
    wupd_hbm,
    wdec_hbm,
    wout_hbm,
    out_ref,
    state_ref,
    x,
    wg,
    ws,
    sector_of,
    node_of,
    wn,
    links_of,
    wsrc,
    wtgt,
    wupd,
    wdec,
    wout,
    hidden,
    message,
    part,
    part_in,
    table,
    reply_all,
    base,
    load_sem,
    part_send,
    part_recv,
    halo_send,
    halo_recv,
    reply_send,
    reply_recv,
):
    band = lax.axis_index("lat")
    sector = lax.axis_index("lon")
    points = x.shape[1]
    latent = ws.shape[0]
    half = latent // 2
    layers = wsrc.shape[0]
    nodes = state_ref.shape[0]
    rows = reply_all.shape[1]
    has_low = band > 0
    has_high = band < n_lat - 1
    side = 1 - 2 * lax.rem(sector, 2)
    columns = (0, side, -side)

    loads = [
        pltpu.make_async_copy(source, target, load_sem.at[i])
        for i, (source, target) in enumerate(
            (
                (x_hbm, x),
                (wg_hbm, wg),
                (ws_hbm, ws),
                (sector_hbm, sector_of),
                (node_hbm, node_of),
                (links_hbm, links_of),
                (wout_hbm, wout),
                (wn_hbm, wn),
                (wsrc_hbm, wsrc),
                (wtgt_hbm, wtgt),
                (wupd_hbm, wupd),
                (wdec_hbm, wdec),
            )
        )
    ]
    for load in loads:
        load.start()

    def beside(lat_step, lon_step):
        return (band + lat_step, lax.rem(sector + lon_step + n_lon, n_lon))

    direct = [column for column in (0, 2, 1) if column not in relayed]
    barrier = pltpu.get_barrier_semaphore()
    for step in range(1, n_lon):
        pl.semaphore_signal(barrier, inc=1, device_id=beside(0, step), device_id_type=MESH)

    @pl.when(has_low)
    def _():
        for column in direct:
            pl.semaphore_signal(
                barrier, inc=1, device_id=beside(-1, columns[column]), device_id_type=MESH
            )

    @pl.when(has_high)
    def _():
        for column in direct:
            pl.semaphore_signal(
                barrier, inc=1, device_id=beside(1, columns[column]), device_id_type=MESH
            )

    zeros = jnp.zeros((3, 2 * nodes, half), BF16)

    @pl.when(band == 0)
    def _():
        for layer in range(layers):
            table[layer, 0:3] = zeros

    @pl.when(band == n_lat - 1)
    def _():
        for layer in range(layers):
            table[layer, 6:9] = zeros

    loads[0].wait()
    loads[1].wait()
    hidden[...] = silu(matmul(x[...], wg[...], 0, 0)).astype(BF16)
    loads[2].wait()
    for start in range(0, points, chunk):
        span = pl.ds(start, chunk)
        message[span, :] = silu(matmul(hidden[span, :], ws[...])).astype(BF16)
    loads[3].wait()
    loads[4].wait()
    target = sector_of[...] * nodes + node_of[...]
    chosen = jnp.where(
        lax.broadcasted_iota(jnp.int32, (n_lon * nodes, points), 0) == target, 1.0, 0.0
    ).astype(BF16)
    partial = matmul(chosen, message[...])
    for other in range(n_lon):
        block = partial[other * nodes : (other + 1) * nodes]
        part[other] = jnp.concatenate([block[:, :half], block[:, half:]], axis=0).astype(BF16)

    inner = jnp.logical_and(has_low, has_high)

    @pl.when(inner)
    def _():
        pl.semaphore_wait(barrier, n_lon - 1 + 2 * len(direct))

    @pl.when(jnp.logical_not(inner))
    def _():
        pl.semaphore_wait(barrier, n_lon - 1 + len(direct))

    sends = []
    for step in range(1, n_lon):
        copy = pltpu.make_async_remote_copy(
            src_ref=part.at[lax.rem(sector + step, n_lon)],
            dst_ref=part_in.at[step - 1],
            send_sem=part_send.at[step - 1],
            recv_sem=part_recv.at[step - 1],
            device_id=beside(0, step),
            device_id_type=MESH,
        )
        copy.start()
        sends.append(copy)

    loads[5].wait()
    loads[6].wait()
    base[...] = matmul(wout[...], hidden[...], 1, 1)
    degree = links_of.shape[0]
    links = jnp.swapaxes(jnp.concatenate([links_of[k] for k in range(degree)], axis=0), 0, 1)
    links = jnp.concatenate([links[:, k : k + 1] for k in range(degree)], axis=0)
    cell = links // nodes
    lon_step = cell % 3 - 1
    column = jnp.where(lon_step == 0, 0, jnp.where(lon_step == side, 1, 2))
    links = links - cell * nodes + ((cell // 3) * 3 + column) * (2 * nodes)
    slots = lax.broadcasted_iota(jnp.int32, (degree * nodes, 6 * nodes), 1)
    wanted = [
        [
            jnp.where(slots == links + (shift - row * 6) * nodes, 1.0, 0.0).astype(BF16)
            for shift in (0, 1)
        ]
        for row in range(3)
    ]
    answered = sector_of[...] * rows + node_of[...]
    fetching = jnp.where(
        lax.broadcasted_iota(jnp.int32, (n_lon * rows, points), 0) == answered, 1.0, 0.0
    ).astype(BF16)

    gathered = part[sector].astype(jnp.float32)
    for load in loads[7:]:
        load.wait()
    for step in range(1, n_lon):
        sends[step - 1].wait_recv()
        gathered = gathered + part_in[step - 1].astype(jnp.float32)
    gathered = jnp.concatenate([gathered[:nodes], gathered[nodes:]], axis=1)
    state = silu(matmul(layer_norm(gathered).astype(BF16), wn[...])).astype(BF16)

    def halo(layer, lat_step, column, source=3):
        slot = (1 - lat_step) * 3 + column
        return pltpu.make_async_remote_copy(
            src_ref=table.at[layer, source],
            dst_ref=table.at[layer, slot],
            send_sem=halo_send.at[layer, slot],
            recv_sem=halo_recv.at[layer, slot],
            device_id=beside(lat_step, columns[column]),
            device_id_type=MESH,
        )

    def forward(layer, row, column):
        slot = row * 3 + column
        return pltpu.make_async_remote_copy(
            src_ref=table.at[layer, row * 3],
            dst_ref=table.at[layer, slot],
            send_sem=halo_send.at[layer, slot],
            recv_sem=halo_recv.at[layer, slot],
            device_id=beside(0, columns[column]),
            device_id_type=MESH,
        )

    for layer in range(layers):
        own = matmul(state, wsrc[layer])
        table[layer, 3] = jnp.concatenate([own[:, :half], own[:, half:]], axis=0).astype(BF16)

        @pl.when(has_high)
        def _():
            for column in direct:
                halo(layer, 1, column).start()

        @pl.when(has_low)
        def _():
            for column in direct:
                halo(layer, -1, column).start()

        for column in (2, 1):
            halo(layer, 0, column).start()
        toward = matmul(state, wtgt[layer])

        @pl.when(has_low)
        def _():
            halo(layer, 1, 0).wait_recv()
            for column in relayed:
                forward(layer, 0, column).start()

        @pl.when(has_high)
        def _():
            halo(layer, -1, 0).wait_recv()
            for column in relayed:
                forward(layer, 2, column).start()

        def pick(row):
            senders = table[layer, 3 * row : 3 * row + 3].reshape(6 * nodes, half)
            return [matmul(which, senders) for which in wanted[row]]

        for column in (1, 2):
            halo(layer, 0, column).wait_recv()
        picks = [pick(1)]

        @pl.when(has_low)
        def _():
            for column in (2, 1):
                halo(layer, 1, column).wait_recv()

        picks.append(pick(0))

        @pl.when(has_high)
        def _():
            for column in (2, 1):
                halo(layer, -1, column).wait_recv()

        picks.append(pick(2))
        picked = jnp.concatenate(
            [picks[0][i] + picks[1][i] + picks[2][i] for i in (0, 1)], axis=1
        )
        summed = silu(picked[0:nodes] + toward)
        for k in range(1, degree):
            summed = summed + silu(picked[k * nodes : (k + 1) * nodes] + toward)
        lifted = layer_norm(summed).astype(BF16)
        state = (state.astype(jnp.float32) + matmul(lifted, wupd[layer])).astype(BF16)

    reply = silu(matmul(state, wdec[...])).astype(BF16)
    reply = matmul(reply, wout[...], 1, 1)
    if rows > nodes:
        filler = jnp.zeros((rows - nodes, reply.shape[1]), jnp.float32)
        reply = jnp.concatenate([reply, filler], axis=0)
    reply_all[sector] = reply.astype(BF16)
    replies = []
    for step in range(1, n_lon):
        copy = pltpu.make_async_remote_copy(
            src_ref=reply_all.at[sector],
            dst_ref=reply_all.at[sector],
            send_sem=reply_send.at[step - 1],
            recv_sem=reply_recv.at[step - 1],
            device_id=beside(0, step),
            device_id_type=MESH,
        )
        copy.start()
        replies.append(copy)
    state_ref[...] = state
    for copy in sends:
        copy.wait_send()
    for layer in range(layers):
        for column in (1, 2):
            halo(layer, 0, column).wait_send()

        @pl.when(has_low)
        def _():
            for column in direct:
                halo(layer, -1, column).wait_send()
            for column in relayed:
                forward(layer, 0, column).wait_send()

        @pl.when(has_high)
        def _():
            for column in direct:
                halo(layer, 1, column).wait_send()
            for column in relayed:
                forward(layer, 2, column).wait_send()

    for step in range(1, n_lon):
        source = lax.rem(sector - step + n_lon, n_lon)
        pltpu.make_async_remote_copy(
            src_ref=reply_all.at[source],
            dst_ref=reply_all.at[source],
            send_sem=reply_send.at[step - 1],
            recv_sem=reply_recv.at[step - 1],
            device_id=beside(0, step),
            device_id_type=MESH,
        ).wait_recv()
    fetched = matmul(reply_all[...].reshape(n_lon * rows, -1), fetching, 0, 0)
    out_ref[...] = (base[...] + fetched).astype(BF16)
    for copy in replies:
        copy.wait_send()


def body(
    grid_input,
    w_grid,
    w_send,
    to_sector,
    to_node,
    w_node,
    mesh_links,
    w_source,
    w_target,
    w_update,
    w_decode,
    w_output,
):
    n_lat = lax.axis_size("lat")
    n_lon = lax.axis_size("lon")
    points, variables = grid_input.shape[2:]
    latent = w_send.shape[0]
    nodes = mesh_links.shape[2]
    layers = w_source.shape[0]
    rows = -(-nodes // 16) * 16
    chunk = points // 3 if points % 48 == 0 else points
    hbm = pl.BlockSpec(memory_space=pltpu.HBM)
    vmem = pl.BlockSpec(memory_space=pltpu.VMEM)
    square = pltpu.VMEM((latent, latent), BF16)
    cube = pltpu.VMEM((layers, latent, latent), BF16)
    result, state = pl.pallas_call(
        functools.partial(kernel, n_lat, n_lon, RELAYED, chunk),
        out_shape=(
            pltpu.VMEM((variables, points), BF16),
            pltpu.VMEM((nodes, latent), BF16),
        ),
        in_specs=[hbm] * 12,
        out_specs=(vmem, vmem),
        scratch_shapes=[
            pltpu.VMEM((variables, points), BF16),
            pltpu.VMEM((variables, latent), BF16),
            square,
            pltpu.VMEM((1, points), jnp.int32),
            pltpu.VMEM((1, points), jnp.int32),
            square,
            pltpu.VMEM((mesh_links.shape[3], 1, nodes), jnp.int32),
            cube,
            cube,
            cube,
            square,
            pltpu.VMEM((variables, latent), BF16),
            pltpu.VMEM((points, latent), BF16),
            pltpu.VMEM((points, latent), BF16),
            pltpu.VMEM((n_lon, 2 * nodes, latent // 2), BF16),
            pltpu.VMEM((n_lon - 1, 2 * nodes, latent // 2), BF16),
            pltpu.VMEM((layers, 9, 2 * nodes, latent // 2), BF16),
            pltpu.VMEM((n_lon, rows, variables), BF16),
            pltpu.VMEM((variables, points), jnp.float32),
            pltpu.SemaphoreType.DMA((12,)),
            pltpu.SemaphoreType.DMA((n_lon - 1,)),
            pltpu.SemaphoreType.DMA((n_lon - 1,)),
            pltpu.SemaphoreType.DMA((layers, 9)),
            pltpu.SemaphoreType.DMA((layers, 9)),
            pltpu.SemaphoreType.DMA((n_lon - 1,)),
            pltpu.SemaphoreType.DMA((n_lon - 1,)),
        ],
        compiler_params=pltpu.CompilerParams(
            collective_id=0, has_side_effects=True, vmem_limit_bytes=LIMIT * 1024 * 1024
        ),
    )(
        jnp.swapaxes(grid_input.reshape(points, variables), 0, 1),
        w_grid,
        w_send,
        to_sector.reshape(1, points),
        to_node.reshape(1, points),
        w_node,
        jnp.transpose(mesh_links, (0, 3, 1, 2)).reshape(-1, 1, nodes),
        w_source,
        w_target,
        w_update,
        w_decode,
        jnp.swapaxes(w_output, 0, 1),
    )
    return (jnp.swapaxes(result, 0, 1).reshape(1, 1, points, variables), state.reshape(1, 1, nodes, latent))


def solution(mesh):
    placed = (
        P("lat", "lon", None, None),
        P(),
        P(),
        P("lat", "lon", None, None),
        P("lat", "lon", None),
        P(),
        P("lat", "lon", None, None),
        P(),
        P(),
        P(),
        P(),
        P(),
    )
    return jax.shard_map(
        body,
        mesh=mesh,
        in_specs=placed,
        out_specs=(P("lat", "lon", None, None), P("lat", "lon", None, None)),
        check_vma=False,
    )
```
